512 devices in a mesh: lhs: 32 (over z_hi, y, core), rhs: 16 (over z_lo, x).
Axes of the slice: x: 4, y: 8, z: 8 (z_hi: 2, z_lo: 4; z = z_hi * 4 + z_lo), core: 2. Of those that a mesh axis runs over, the one named last changes fastest.
Arguments:
- left_table: float32 [32, 16, 384, 400], P('lhs', 'rhs'), may hold values from -6 to 6
- left_state: float32 [32, 16, 384], P('lhs', 'rhs'), may hold values from 1e-06 to 0.0001
- right_table: float32 [32, 16, 384, 400], P('lhs', 'rhs'), may hold values from -6 to 6
- right_state: float32 [32, 16, 384], P('lhs', 'rhs'), may hold values from 1e-06 to 0.0001
- operators: float32 [2, 400, 400], replicated, may hold values from -0.3125 to 0.3125
- operator_state: float32 [2, 400], replicated, may hold values from 0.1 to 10
- sources: int32 [32, 16, 384], P('lhs', 'rhs'), may hold values from 0 to 383
- targets: int32 [32, 16, 384], P('lhs', 'rhs'), may hold values from 0 to 383
- relations: int32 [32, 16, 384], P('lhs', 'rhs'), may hold values from 0 to 1, as said below
- negatives: int32 [32, 16, 384], P('lhs', 'rhs'), may hold values from 0 to 383
- counts: int32 [32, 16], P('lhs', 'rhs'), may hold values from 1 to 384, 3840 in all within a row
Outputs:
- new_left: float32 [32, 16, 384, 400], P('lhs', 'rhs')
- new_right: float32 [32, 16, 384, 400], P('lhs', 'rhs')
- new_operators: float32 [2, 400, 400], replicated
The draws below stay inside these ranges and needn't reach their ends.
Inputs may be any that keep to these rules, and one draw needn't show every extreme that they name: For each index along lhs, the counts over rhs sum to 3840, and at least one of them equals 384. `relations`: within each bucket the edge slots are grouped by relation: relation ids never fall from one slot to the next.
All inputs are finite; a program needn't handle non-finite values. No bound on the sum of `counts` on one device may be relied on, other than what follows from the above.
Results may differ from the reference program's by a relative error of at most 0.0003.
Values sent between devices are 32-bit elements; how exact they have to be, the bound alone decides.
A program may use at most 64 MiB of HBM per device.

```python
import math
import jax
import jax.numpy as jnp
import numpy as np
from jax import lax

WIDTH = 400
RELATION_TYPES = 2
SAMPLES = 384
ROWS = 384
EDGES = 384
BUCKET_TOTAL = 3840
N_LHS = 32
N_RHS = 16


def draw_relations(key, part):
    key = jax.random.fold_in(key, 7)
    split_at = jax.random.randint(key, (N_LHS, N_RHS, 1), 0, EDGES + 1)
    slots = jnp.arange(EDGES, dtype=jnp.int32)
    return (slots[None, None, :] >= split_at).astype(jnp.int32)


def touch_ends(values, stream_key, low, top_value):
    shape = values.shape
    place = [jax.random.randint(jax.random.fold_in(stream_key, axis), (), 0, shape[axis]) for axis in range(len(shape))]
    values = values.at[tuple(place)].set(low)
    longest = shape.index(max(shape))
    place[longest] = (place[longest] + 1) % shape[longest]
    return values.at[tuple(place)].set(top_value)


def block_levels(key, extent, split, low, largest):
    def one(dim, shards_of):
        heights = jax.random.uniform(jax.random.fold_in(jax.random.fold_in(key, 6), dim), (shards_of,), jnp.float32, low / len(split), largest / len(split))
        return jnp.repeat(jnp.exp(heights), extent[dim] // shards_of).reshape((-1,) + (1,) * (len(extent) - dim - 1))

    gain = one(*split[0])
    for cut in split[1:]:
        gain = gain * one(*cut)
    return gain


def split_up(amount, total, most, lean):
    portions = [(1 << 20) // math.isqrt(standing ** lean) + 1 for standing in range(2, amount + 1)]
    surplus, given = total - most - (amount - 1), [1] * (amount - 1)
    while surplus > 0:
        candidates = [i for i in range(amount - 1) if given[i] < most]
        whole, budget = sum([portions[i] for i in candidates]), surplus
        for i in candidates:
            extra = min(most - given[i], max(1, budget * portions[i] // whole), surplus)
            given[i] = given[i] + extra
            surplus = surplus - extra
    return np.array([most] + given)


def ragged(key, number_of, total, reach, skew):
    if number_of == 2:
        one = jax.random.randint(key, (), max(1, total - reach), min(reach, total - 1) + 1)
        return jnp.stack([one, total - one])
    tallies = jnp.asarray(split_up(number_of, total, reach, skew), jnp.int32)
    couples = (number_of - 1) // 2
    giver, sink = tallies[1:1 + 2 * couples:2], tallies[2:2 + 2 * couples:2]
    slack = jnp.minimum(giver - 1, reach - sink)
    passed = jax.random.randint(jax.random.fold_in(key, 1), (couples,), 0, 1 << 20) % (slack + 1)
    tallies = tallies.at[1:1 + 2 * couples:2].set(giver - passed).at[2:2 + 2 * couples:2].set(sink + passed)
    return tallies[jax.random.permutation(jax.random.fold_in(key, 2), number_of)]


def normal_values(rng, shape, deviation, bound, split=(), held_as=jnp.bfloat16):
    loudness = block_levels(rng, shape, split, -0.22, 0.18) if split else 1.0
    entries = jax.random.normal(rng, shape, jnp.float32) * deviation * loudness
    return jnp.minimum(jnp.maximum(entries, -bound), bound).astype(held_as)


def setup_inputs(seed: int = 0) -> dict:
    keys = jax.random.split(jax.random.key(seed), 12)
    return {
        "left_table": normal_values(keys[0], (N_LHS, N_RHS, ROWS, WIDTH), 1.0, 6.0, ((0, 32), (1, 16)), jnp.float32),
        "left_state": jnp.clip(jnp.exp(math.log(0.0001) - 4.6051702 * jax.random.uniform(keys[1], (N_LHS, N_RHS, ROWS), jnp.float32) ** block_levels(keys[1], (N_LHS, N_RHS, ROWS), ((0, 32), (1, 16)), -0.2, 0.2)), 9.999999974752427e-07, 0.0001),
        "right_table": normal_values(keys[2], (N_LHS, N_RHS, ROWS, WIDTH), 1.0, 6.0, ((0, 32), (1, 16)), jnp.float32),
        "right_state": jnp.clip(jnp.exp(math.log(0.0001) - 4.6051702 * jax.random.uniform(keys[3], (N_LHS, N_RHS, ROWS), jnp.float32) ** block_levels(keys[3], (N_LHS, N_RHS, ROWS), ((0, 32), (1, 16)), -0.2, 0.2)), 9.999999974752427e-07, 0.0001),
        "operators": normal_values(keys[4], (RELATION_TYPES, WIDTH, WIDTH), WIDTH ** -0.5, 0.3125, (), jnp.float32),
        "operator_state": jnp.clip(jnp.exp(jax.random.uniform(keys[5], (RELATION_TYPES, WIDTH), jnp.float32, math.log(0.1), math.log(10.0))), 0.1, 10.0),
        "sources": touch_ends(jax.random.randint(keys[6], (N_LHS, N_RHS, EDGES), 0, ROWS), jax.random.fold_in(keys[6], 1), 0, ROWS - 1).astype(jnp.int32),
        "targets": touch_ends(jax.random.randint(keys[7], (N_LHS, N_RHS, EDGES), 0, ROWS), jax.random.fold_in(keys[7], 1), 0, ROWS - 1).astype(jnp.int32),
        "relations": draw_relations(jax.random.fold_in(keys[11], 71), 0),
        "negatives": touch_ends(jax.random.randint(keys[9], (N_LHS, N_RHS, SAMPLES), 0, ROWS), jax.random.fold_in(keys[9], 1), 0, ROWS - 1).astype(jnp.int32),
        "counts": jax.vmap(lambda own: ragged(own, N_RHS, BUCKET_TOTAL, EDGES, 2))(jax.random.split(keys[10], N_LHS)).reshape((N_LHS, N_RHS)).astype(jnp.int32),
    }


def bucket_loss(left_block, right_block, operators, sources, targets, relations, negatives, live_count):
    inputs = left_block[sources]
    mapped_all = jnp.einsum('ew,rwv->erv', inputs, operators, precision=lax.Precision.HIGHEST)
    kind_ids = jnp.arange(operators.shape[0], dtype=jnp.int32)
    select = (relations[:, None] == kind_ids[None, :]).astype(jnp.float32)
    mapped = lax.optimization_barrier(jnp.sum(mapped_all * select[:, :, None], axis=1))
    unit_mapped = mapped * lax.rsqrt(lax.optimization_barrier(jnp.sum(mapped * mapped, -1, keepdims=True)) + 1e-06)
    unit_right = right_block * lax.rsqrt(lax.optimization_barrier(jnp.sum(right_block * right_block, -1, keepdims=True)) + 1e-06)
    positive = lax.optimization_barrier(jnp.sum(unit_mapped * unit_right[targets], -1))
    sampled = jnp.dot(unit_mapped, unit_right[negatives].T, precision=lax.Precision.HIGHEST)
    log_total = jnp.log(jnp.exp(positive) + lax.optimization_barrier(jnp.sum(jnp.exp(sampled), -1)))
    live_slot = jnp.arange(sources.shape[0], dtype=jnp.int32) < live_count
    return jnp.sum(jnp.where(live_slot, log_total - positive, jnp.zeros_like(log_total)))

def adagrad(weights, sums_in, gradient):
    summed = sums_in + lax.optimization_barrier(jnp.mean(gradient * gradient, -1))
    return weights - 0.1 * gradient / jnp.sqrt(summed)[..., None]

def reference(left_table, left_state, right_table, right_state, operators, operator_state, sources, targets, relations, negatives, counts):
    devices = N_LHS * N_RHS
    left_window = jnp.roll(left_table, 1, axis=0).reshape(devices, ROWS, WIDTH)
    left_wstate = jnp.roll(left_state, 1, axis=0).reshape(devices, ROWS)
    right_window = jnp.roll(right_table, 1, axis=1).reshape(devices, ROWS, WIDTH)
    right_wstate = jnp.roll(right_state, 1, axis=1).reshape(devices, ROWS)
    scan_items = (left_window, right_window, sources.reshape(devices, EDGES), targets.reshape(devices, EDGES), relations.reshape(devices, EDGES), negatives.reshape(devices, SAMPLES), counts.reshape(devices))

    def visit_bucket(summed, bucket_item):
        left_block, right_block, src_rows, dst_rows, kind_rows, neg_rows, live_count = bucket_item

        def local_loss(first, second, third):
            return bucket_loss(first, second, third, src_rows, dst_rows, kind_rows, neg_rows, live_count)
        loss_value, pullback = jax.vjp(local_loss, left_block, right_block, operators)
        left_grad, right_grad, operator_grad = pullback(jnp.ones_like(loss_value))
        return (summed + operator_grad, (left_grad, right_grad))
    operator_grad, row_grads = lax.scan(visit_bucket, jnp.zeros_like(operators), scan_items)
    new_left = adagrad(left_window, left_wstate, row_grads[0]).reshape(N_LHS, N_RHS, ROWS, WIDTH)
    new_right = adagrad(right_window, right_wstate, row_grads[1]).reshape(N_LHS, N_RHS, ROWS, WIDTH)
    new_operators = adagrad(operators, operator_state, operator_grad)
    return (new_left, new_right, new_operators)
```

```python
import functools

import jax
import jax.numpy as jnp
from jax import lax
from jax.experimental import pallas as pl
from jax.experimental.pallas import tpu as pltpu
from jax.sharding import PartitionSpec as P

MESH = pl.DeviceIdType.MESH
F32 = jnp.float32
BF16 = jnp.bfloat16

ROWS = 384
WIDTH = 400
LANES = 512
NX, NY, NZ = 4, 8, 8

X0, XC = 0, 48
Y0, YC = 192, 16
Z0, ZC = 320, 16
PADDED = 448

NN = (((1,), (0,)), ((), ()))
NT = (((1,), (1,)), ((), ()))


def split(value):
    high = value.astype(BF16)
    return high, (value - high.astype(F32)).astype(BF16)


def dot(a, b, dims=NN):
    return lax.dot_general(a, b, dims, preferred_element_type=F32)


def dot3(a, b, dims=NN):
    (a_high, a_low), (b_high, b_low) = a, b
    return dot(a_high, b_high, dims) + (dot(a_high, b_low, dims) + dot(a_low, b_high, dims))


def device(x, y, z, c):
    return ((z // 4) * 16 + y * 2 + c, (z % 4) * 4 + x)


def adagrad(weights, sums, gradient):
    summed = sums + jnp.sum(gradient * gradient, -1, keepdims=True) * (1.0 / WIDTH)
    return weights - gradient * (0.1 / jnp.sqrt(summed))


def kernel(
    left_ref, lstate_ref, right_ref, rstate_ref, ops_ref, opstate_ref,
    src_ref, tgt_ref, rel_ref, neg_ref, cnt_ref,
    new_left_ref, new_right_ref, new_ops_ref,
    left, right, lstate, rstate, ops, out_left, out_right, out_ops, rows8, state8,
    grad, sibling, total,
    rx, ry, rz, qx, qy, qz, r2x, r2y, r2z, r3x, r3y, r3z, fx, fy, fz,
    perm_send, perm_recv, local_sem, out_sem,
    core_send, core_recv, s1, v1, s2, v2, s3, v3, s4, v4, s5, v5, s6, v6,
):
    lhs, rhs = lax.axis_index("lhs"), lax.axis_index("rhs")
    mx, my, mz, mc = rhs % 4, (lhs // 2) % 8, (lhs // 16) * 4 + rhs // 4, lhs % 2
    other = 1 - mc

    def along(axis, steps):
        if axis == "x":
            return device((mx + steps) % NX, my, mz, mc)
        if axis == "y":
            return device(mx, (my + steps) % NY, mz, mc)
        return device(mx, my, (mz + steps) % NZ, mc)

    pair = device(mx, my, mz, other)
    lhs_next, lhs_prev = ((lhs + 1) % 32, rhs), ((lhs + 31) % 32, rhs)
    rhs_next, rhs_prev = (lhs, (rhs + 1) % 16), (lhs, (rhs + 15) % 16)
    size = {"x": NX, "y": NY, "z": NZ}
    me = {"x": mx, "y": my, "z": mz}

    ops_copy = pltpu.make_async_copy(ops_ref, ops, local_sem.at[0])
    ops_copy.start()

    peers = [lhs_next, lhs_prev, rhs_next, rhs_prev, pair]
    peers += [along(axis, steps) for axis in "xyz" for steps in range(1, size[axis])]
    barrier = pltpu.get_barrier_semaphore()
    for peer in peers:
        pl.semaphore_signal(barrier, inc=1, device_id=peer, device_id_type=MESH)
    pl.semaphore_wait(barrier, len(peers))

    def send(src, dst, ssem, rsem, target):
        copy = pltpu.make_async_remote_copy(
            src_ref=src, dst_ref=dst, send_sem=ssem, recv_sem=rsem, device_id=target, device_id_type=MESH
        )
        copy.start()
        return copy

    right_copy = send(right_ref, right, perm_send.at[0], perm_recv.at[0], rhs_next)
    left_copy = send(left_ref, left, perm_send.at[1], perm_recv.at[1], lhs_next)
    rstate_copy = send(rstate_ref, rstate, perm_send.at[2], perm_recv.at[2], rhs_next)
    lstate_copy = send(lstate_ref, lstate, perm_send.at[3], perm_recv.at[3], lhs_next)

    grad[...] = jnp.zeros_like(grad)
    rows8[0:1, :] = src_ref[...].astype(F32)
    rows8[1:2, :] = tgt_ref[...].astype(F32)
    rows8[2:3, :] = rel_ref[...].astype(F32)
    rows8[3:4, :] = neg_ref[...].astype(F32)
    rows8[4:8, :] = jnp.zeros((4, ROWS), F32)
    columns = rows8[...].T
    lane = lax.broadcasted_iota(jnp.int32, (ROWS, ROWS), 1).astype(F32)
    sublane = lax.broadcasted_iota(jnp.int32, (ROWS, ROWS), 0).astype(F32)
    hot_src = (columns[:, 0:1] == lane).astype(F32).astype(BF16)
    hot_src_t = (rows8[0:1, :] == sublane).astype(F32).astype(BF16)
    hot_tgt = (columns[:, 1:2] == lane).astype(F32)
    hot_neg = (columns[:, 3:4] == lane).astype(F32)
    multiplicity = jnp.sum(hot_neg, axis=0, keepdims=True)
    rel = columns[:, 2:3]
    edge = lax.broadcasted_iota(jnp.int32, (ROWS, 1), 0)
    live = (edge < cnt_ref[...]).astype(F32)
    state8[...] = jnp.zeros_like(state8)
    state8[0:2, 0:WIDTH] = opstate_ref[...]
    op_sums = state8[...].T
    ops_copy.wait()
    ops_split = [split(ops[r]) for r in range(2)]

    left_copy.wait_recv()
    left_high, left_low = split(left[...])
    in_high, in_low = dot(hot_src, left_high).astype(BF16), dot(hot_src, left_low).astype(BF16)
    inputs = (in_high, in_low)
    mapped = jnp.where(rel < 0.5, dot3(inputs, ops_split[0]), dot3(inputs, ops_split[1]))
    inv_mapped = lax.rsqrt(jnp.sum(mapped * mapped, -1, keepdims=True) + 1e-06)
    unit_mapped = mapped * inv_mapped
    unit_split = split(unit_mapped)
    inputs_t = (in_high.astype(F32).T.astype(BF16), in_low.astype(F32).T.astype(BF16))

    right_copy.wait_recv()
    right_block = right[...]
    inv_right = lax.rsqrt(jnp.sum(right_block * right_block, -1, keepdims=True) + 1e-06)
    unit_right = right_block * inv_right
    right_split = split(unit_right)
    scores = dot3(unit_split, right_split, NT)
    positive = jnp.exp(jnp.sum(hot_tgt * scores, -1, keepdims=True))
    weights = multiplicity * jnp.exp(scores)
    norm = positive + jnp.sum(weights, -1, keepdims=True)
    scale = live / norm
    pull = weights * scale + hot_tgt * (positive * scale - live)
    pull_split = split(pull)
    d_unit = dot3(pull_split, right_split)
    d_mapped = inv_mapped * (d_unit - unit_mapped * jnp.sum(unit_mapped * d_unit, -1, keepdims=True))

    def operator_grad(kind):
        picked = jnp.where(rel == kind.astype(F32), d_mapped, 0.0)
        return dot3(inputs_t, split(picked))

    grad[0, 0:WIDTH, 0:WIDTH] = operator_grad(other)
    pair_copy = send(grad.at[0], sibling, core_send.at[0], core_recv.at[0], pair)
    own = operator_grad(mc)
    grad[1, 0:WIDTH, 0:WIDTH] = own
    pair_copy.wait_recv()
    total[...] = grad[1] + sibling[...]

    first = (("x", X0, XC, rx, 0), ("y", Y0, YC, ry, 3), ("z", Z0, ZC, rz, 10))
    copies1 = []
    for axis, start, rows, slots, base in first:
        for steps in range(1, size[axis]):
            to = (me[axis] + steps) % size[axis]
            chunk = total.at[pl.ds(pl.multiple_of(start + to * rows, 8), rows)]
            copies1.append(
                send(chunk, slots.at[steps - 1], s1.at[base + steps - 1], v1.at[base + steps - 1], along(axis, steps))
            )

    rstate_copy.wait_recv()
    lstate_copy.wait_recv()
    rows8[4:5, :] = lstate[...]
    rows8[5:6, :] = rstate[...]
    sums = rows8[...].T
    d_right_unit = dot3(split(pull.T), unit_split)
    d_right = inv_right * (
        d_right_unit - unit_right * jnp.sum(unit_right * d_right_unit, -1, keepdims=True)
    )
    out_right[...] = adagrad(right_block, sums[:, 5:6], d_right)
    right_out = pltpu.make_async_copy(out_right, new_right_ref, out_sem.at[0])
    right_out.start()
    d_inputs = dot3(split(jnp.where(rel < 0.5, d_mapped, 0.0)), ops_split[0], NT) + dot3(
        split(jnp.where(rel < 0.5, 0.0, d_mapped)), ops_split[1], NT
    )
    d_high, d_low = split(d_inputs)
    d_left = dot(hot_src_t, d_high) + dot(hot_src_t, d_low)
    out_left[...] = adagrad(left[...], sums[:, 4:5], d_left)
    left_out = pltpu.make_async_copy(out_left, new_left_ref, out_sem.at[1])
    left_out.start()

    def summed(start, rows, slots, count):
        value = total[pl.ds(pl.multiple_of(start, 8), rows), :]
        for slot in range(count):
            value = value + slots[slot]
        return value

    copies2 = []
    second = (("y", qx, r2x, 0), ("z", qy, r2y, 7), ("y", qz, r2z, 14))
    for part, (axis1, start, rows, slots, base1) in enumerate(first):
        axis, pieces, _, base = second[part]
        for steps in range(1, size[axis1]):
            copies1[base1 + steps - 1].wait_recv()
        value = summed(start + me[axis1] * rows, rows, slots, size[axis1] - 1)
        half = rows // 2
        for j in range(8):
            pieces[j] = value[half * (j // 4):half * (j // 4 + 1), 128 * (j % 4):128 * (j % 4 + 1)]
        for steps in range(1, size[axis]):
            to = (me[axis] + steps) % size[axis]
            k = base + steps - 1
            copies2.append(send(pieces.at[to], second[part][2].at[steps - 1], s2.at[k], v2.at[k], along(axis, steps)))

    third = (("z", r3x, 0), ("x", r3y, 7), ("x", r3z, 10))
    copies3 = []
    for part, (axis2, pieces, slots2, base2) in enumerate(second):
        axis, slots, base = third[part]
        for steps in range(1, size[axis2]):
            copies2[base2 + steps - 1].wait_recv()
        value = pieces[me[axis2]]
        for slot in range(size[axis2] - 1):
            value = value + slots2[slot]
        slots[me[axis]] = value
        for steps in range(1, size[axis]):
            k = base + steps - 1
            copies3.append(
                send(slots.at[me[axis]], slots.at[me[axis]], s3.at[k], v3.at[k], along(axis, steps))
            )

    finals = (fx, fy, fz)
    copies4 = []
    for part, (axis3, slots, base3) in enumerate(third):
        axis1, axis2 = first[part][0], second[part][0]
        base = second[part][3]
        for steps in range(1, size[axis3]):
            copies3[base3 + steps - 1].wait_recv()
        value = slots[0]
        for slot in range(1, size[axis3]):
            value = value + slots[slot]
        final = finals[part]
        final[mc, me[axis1], me[axis2]] = value
        for steps in range(1, size[axis2]):
            k = base + steps - 1
            piece = final.at[mc, me[axis1], me[axis2]]
            copies4.append(send(piece, piece, s4.at[k], v4.at[k], along(axis2, steps)))

    copies5, copies6 = [], []
    for part, (axis1, _, _, _, base1) in enumerate(first):
        axis2, base2 = second[part][0], second[part][3]
        final = finals[part]
        for steps in range(1, size[axis2]):
            copies4[base2 + steps - 1].wait_recv()
        chunk = final.at[mc, me[axis1]]
        for steps in range(1, size[axis1]):
            k = base1 + steps - 1
            copies5.append(send(chunk, chunk, s5.at[k], v5.at[k], along(axis1, steps)))
        copies6.append(send(chunk, chunk, s6.at[part], v6.at[part], pair))
    for part, (axis1, _, _, _, base1) in enumerate(first):
        final = finals[part]
        for steps in range(1, size[axis1]):
            k = base1 + steps - 1
            copies5[k].wait_recv()
            chunk = final.at[mc, (me[axis1] + size[axis1] - steps) % size[axis1]]
            copies6.append(send(chunk, chunk, s6.at[3 + k], v6.at[3 + k], pair))
    for copy in copies6:
        copy.wait_recv()

    for kind in range(2):
        for part, (axis1, start, rows, _, _) in enumerate(first):
            half = rows // 2
            for j in range(size[axis1]):
                for h in range(2):
                    row = start + j * rows + h * half
                    if row >= WIDTH:
                        continue
                    gradient = jnp.concatenate([finals[part][kind, j, 4 * h + q] for q in range(4)], axis=-1)
                    gradient = gradient[:, 0:WIDTH]
                    old = ops[kind, row:row + half, :]
                    out_ops[kind, row:row + half, :] = adagrad(old, op_sums[row:row + half, kind:kind + 1], gradient)
    ops_out = pltpu.make_async_copy(out_ops, new_ops_ref, out_sem.at[2])
    ops_out.start()
    for copy in [right_copy, left_copy, rstate_copy, lstate_copy, pair_copy]:
        copy.wait_send()
    for copy in copies1 + copies2 + copies3 + copies4 + copies5 + copies6:
        copy.wait_send()
    right_out.wait()
    left_out.wait()
    ops_out.wait()


def body(
    left_table, left_state, right_table, right_state, operators, operator_state,
    sources, targets, relations, negatives, counts,
):
    vmem, hbm = pl.BlockSpec(memory_space=pltpu.VMEM), pl.BlockSpec(memory_space=pl.ANY)
    dma = pltpu.SemaphoreType.DMA

    def buf(*shape):
        return pltpu.VMEM(shape, F32)

    block = jax.ShapeDtypeStruct((ROWS, WIDTH), F32)
    new_left, new_right, new_operators = pl.pallas_call(
        kernel,
        out_shape=(block, block, jax.ShapeDtypeStruct((2, WIDTH, WIDTH), F32)),
        in_specs=[hbm, vmem, hbm, vmem, hbm, vmem, vmem, vmem, vmem, vmem, vmem],
        out_specs=(hbm, hbm, hbm),
        scratch_shapes=[
            buf(ROWS, WIDTH), buf(ROWS, WIDTH), buf(1, ROWS), buf(1, ROWS), buf(2, WIDTH, WIDTH),
            buf(ROWS, WIDTH), buf(ROWS, WIDTH), buf(2, WIDTH, WIDTH), buf(8, ROWS), buf(8, LANES),
            buf(2, PADDED, LANES), buf(PADDED, LANES), buf(PADDED, LANES),
            buf(3, XC, LANES), buf(7, YC, LANES), buf(7, ZC, LANES),
            buf(8, XC // 2, 128), buf(8, YC // 2, 128), buf(8, ZC // 2, 128),
            buf(7, XC // 2, 128), buf(7, YC // 2, 128), buf(7, ZC // 2, 128),
            buf(8, XC // 2, 128), buf(4, YC // 2, 128), buf(4, ZC // 2, 128),
            buf(2, 4, 8, XC // 2, 128), buf(2, 8, 8, YC // 2, 128), buf(2, 8, 8, ZC // 2, 128),
            dma((4,)), dma((4,)), dma((1,)), dma((3,)),
            dma((1,)), dma((1,)), dma((17,)), dma((17,)), dma((21,)), dma((21,)),
            dma((13,)), dma((13,)), dma((21,)), dma((21,)), dma((17,)), dma((17,)),
            dma((20,)), dma((20,)),
        ],
        compiler_params=pltpu.CompilerParams(
            collective_id=0, has_side_effects=True, vmem_limit_bytes=48 * 2**20
        ),
        name="bucket_round",
    )(
        left_table.reshape(ROWS, WIDTH), left_state.reshape(1, ROWS),
        right_table.reshape(ROWS, WIDTH), right_state.reshape(1, ROWS),
        operators, operator_state,
        sources.reshape(1, ROWS), targets.reshape(1, ROWS),
        relations.reshape(1, ROWS), negatives.reshape(1, ROWS), counts,
    )
    return new_left[None, None], new_right[None, None], new_operators


def solution(mesh):
    edges = P("lhs", "rhs", None)
    blocks = P("lhs", "rhs", None, None)
    return jax.shard_map(
        body,
        mesh=mesh,
        in_specs=(blocks, edges, blocks, edges, P(), P(), edges, edges, edges, edges, P("lhs", "rhs")),
        out_specs=(blocks, blocks, P()),
        check_vma=False,
    )
```

```python
import functools

import jax
import jax.numpy as jnp
from jax import lax
from jax.experimental import pallas as pl
from jax.experimental.pallas import tpu as pltpu
from jax.sharding import PartitionSpec as P

MESH = pl.DeviceIdType.MESH
F32 = jnp.float32
BF16 = jnp.bfloat16

ROWS = 384
WIDTH = 400
VMEM_BYTES = 64 * 2**20 - 4096
NX, NY, NZ = 4, 8, 8
CUT = 208
PIECES = ((0, 104), (104, 104), (208, 96), (304, 96))

UNITS = 160
XC, YC, ZC = 20, 5, 5
X0, Y0, Z0 = 0, 80, 120

NN = (((1,), (0,)), ((), ()))
NT = (((1,), (1,)), ((), ()))


def split(value):
    high = value.astype(BF16)
    return high, (value - high.astype(F32)).astype(BF16)


def dot(a, b, dims=NN):
    return lax.dot_general(a, b, dims, preferred_element_type=F32)


def dot3(a, b, dims=NN):
    (a_high, a_low), (b_high, b_low) = a, b
    return dot(a_high, b_high, dims) + (dot(a_high, b_low, dims) + dot(a_low, b_high, dims))


def device(x, y, z, c):
    return ((z // 4) * 16 + y * 2 + c, (z % 4) * 4 + x)


def adagrad(weights, sums, gradient, axis):
    summed = sums + jnp.sum(gradient * gradient, axis, keepdims=True) * (1.0 / WIDTH)
    return weights - gradient * (0.1 / jnp.sqrt(summed))


def kernel(
    left_ref, lstate_ref, right_ref, rstate_ref, ops_ref, opstate_hbm,
    src_hbm, tgt_hbm, rel_hbm, neg_hbm, cnt_hbm,
    new_left_ref, new_right_ref, new_ops_ref,
    left, right, lstate, rstate, ops, out_left, out_right, out_ops, rows8, state8, tails, gsum,
    grad, sibling, total,
    rx, ry, rz, qx, qy, qz, r2x, r2y, r2z, r3x, r3y, r3z, fx, fy, fz,
    opstate_ref, src_ref, tgt_ref, rel_ref, neg_ref, cnt_ref,
    perm_send, perm_recv, local_sem, out_sem,
    core_send, core_recv, s1, v1, s2, v2, s3, v3, s4, v4, s5, v5, s6, v6,
):
    lhs, rhs = lax.axis_index("lhs"), lax.axis_index("rhs")
    mx, my, mz, mc = rhs % 4, (lhs // 2) % 8, (lhs // 16) * 4 + rhs // 4, lhs % 2
    other = 1 - mc

    def along(axis, steps):
        if axis == "x":
            return device((mx + steps) % NX, my, mz, mc)
        if axis == "y":
            return device(mx, (my + steps) % NY, mz, mc)
        return device(mx, my, (mz + steps) % NZ, mc)

    pair = device(mx, my, mz, other)
    size = {"x": NX, "y": NY, "z": NZ}
    me = {"x": mx, "y": my, "z": mz}

    peers = [((lhs + 1) % 32, rhs), ((lhs + 31) % 32, rhs), (lhs, (rhs + 1) % 16), (lhs, (rhs + 15) % 16)]
    peers += [pair, (lhs + 15 - 2 * (lhs % 16), rhs)]
    peers += [along(axis, steps) for axis in "xyz" for steps in range(1, size[axis])]
    barrier = pltpu.get_barrier_semaphore()
    for peer in peers:
        pl.semaphore_signal(barrier, inc=1, device_id=peer, device_id_type=MESH)
    place = lhs % 16
    for spot, steps in ((15, (14, 3)), (13, (18, 19)), (2, (29, 30)), (0, (13, 2))):
        @pl.when(place == spot)
        def _():
            for step in steps:
                pl.semaphore_signal(
                    barrier, inc=1, device_id=((lhs + step) % 32, rhs), device_id_type=MESH
                )
    greeted = len(peers) + 2 * ((place == 15) | (place == 13) | (place == 2) | (place == 0)).astype(jnp.int32)
    loads = [
        pltpu.make_async_copy(far, near, local_sem.at[i])
        for i, (far, near) in enumerate((
            (src_hbm, src_ref), (tgt_hbm, tgt_ref), (rel_hbm, rel_ref), (neg_hbm, neg_ref), (cnt_hbm, cnt_ref),
            (opstate_hbm, opstate_ref), (ops_ref, ops),
        ))
    ]
    for load in loads:
        load.start()
    pl.semaphore_wait(barrier, greeted)

    def make(src, dst, ssem, rsem, target):
        return pltpu.make_async_remote_copy(
            src_ref=src, dst_ref=dst, send_sem=ssem, recv_sem=rsem, device_id=target, device_id_type=MESH
        )

    def send(src, dst, ssem, rsem, target):
        copy = make(src, dst, ssem, rsem, target)
        copy.start()
        return copy

    parts = (pl.ds(0, CUT), pl.ds(CUT, WIDTH - CUT))
    corner_r, corner_l = (rhs % 4) == 3, (lhs % 16) == 15
    next_r, next_l = (rhs + 1) % 16, (lhs + 1) % 32
    hop_r = (jnp.where(corner_r, rhs - 3, next_r),) * 2 + (jnp.where(corner_r, (rhs + 4) % 16, next_r),) * 2
    hop_l = (
        next_l,
        jnp.where(corner_l, (lhs + 16) % 32, next_l),
        jnp.where(corner_l, (lhs + 14) % 32, next_l),
        jnp.where(corner_l, (lhs + 3) % 32, next_l),
    )
    slot_r = (corner_r.astype(jnp.int32),) * 4
    slot_l = (0,) + (corner_l.astype(jnp.int32),) * 3
    sent, got_r, got_l = [], {}, {}
    for p in (2, 0, 3, 1):
        part = pl.ds(*PIECES[p])
        sent.append(send(
            left_ref.at[part], left.at[slot_l[p], part],
            perm_send.at[4 + p], perm_recv.at[slot_l[p], 4 + p], (hop_l[p], rhs),
        ))
        sent.append(send(
            right_ref.at[part], right.at[slot_r[p], part],
            perm_send.at[p], perm_recv.at[slot_r[p], p], (lhs, hop_r[p]),
        ))
        got_r[p] = make(right.at[1, part], right.at[0, part], perm_send.at[10 + p], perm_recv.at[0, p], pair)
        got_l[p] = make(left.at[1, part], left.at[0, part], perm_send.at[14 + p], perm_recv.at[0, 4 + p], pair)
    rstate_copy = send(rstate_ref, rstate, perm_send.at[8], perm_recv.at[0, 8], (lhs, next_r))
    lstate_copy = send(lstate_ref, lstate, perm_send.at[9], perm_recv.at[0, 9], (next_l, rhs))
    sent += [rstate_copy, lstate_copy]

    def relay(here, buffer, p, base, target):
        part, sem = pl.ds(*PIECES[p]), perm_send.at[10 + base + p]

        @pl.when(here)
        def _():
            make(buffer.at[0, part], buffer.at[1, part], sem, perm_recv.at[1, base + p], pair).wait_recv()
            make(buffer.at[1, part], buffer.at[0, part], sem, perm_recv.at[0, base + p], target).start()

    def relayed(here, buffer, p, base):
        part, sem = pl.ds(*PIECES[p]), perm_send.at[10 + base + p]

        @pl.when(here)
        def _():
            make(buffer.at[1, part], buffer.at[0, part], sem, perm_recv.at[0, base + p], pair).wait_send()

    relays = [
        (corner_r, right, 2, 0, (lhs, rhs - 3)),
        ((rhs % 4) == 0, right, 0, 0, (lhs, (rhs + 4) % 16)),
        (corner_l, left, 1, 4, (lhs - 15, rhs)),
        ((lhs % 16) == 13, left, 2, 4, (lhs - 13, rhs)),
        ((lhs % 16) == 2, left, 3, 4, (lhs - 2, rhs)),
        (corner_r, right, 3, 0, (lhs, rhs - 3)),
        ((rhs % 4) == 0, right, 1, 0, (lhs, (rhs + 4) % 16)),
    ]

    for load in loads[:6]:
        load.wait()
    rows8[0:1, :] = src_ref[...].astype(F32)
    rows8[1:2, :] = tgt_ref[...].astype(F32)
    rows8[2:3, :] = rel_ref[...].astype(F32)
    rows8[3:4, :] = neg_ref[...].astype(F32)
    rows8[4:8, :] = jnp.zeros((4, ROWS), F32)
    columns = rows8[...].T
    lane = lax.broadcasted_iota(jnp.int32, (ROWS, ROWS), 1).astype(F32)
    sublane = lax.broadcasted_iota(jnp.int32, (ROWS, ROWS), 0).astype(F32)
    hot_src = (columns[:, 0:1] == lane).astype(F32).astype(BF16)
    hot_src_t = (rows8[0:1, :] == sublane).astype(F32).astype(BF16)
    hot_tgt = (columns[:, 1:2] == lane).astype(F32)
    hot_neg = (columns[:, 3:4] == lane).astype(F32)
    multiplicity = jnp.sum(hot_neg, axis=0, keepdims=True)
    rel = rows8[2:3, :]
    edge = lax.broadcasted_iota(jnp.int32, (ROWS, 1), 0)
    live = (edge < cnt_ref[...]).astype(F32)
    state8[...] = jnp.zeros_like(state8)
    state8[0:2, 0:WIDTH] = opstate_ref[...]
    op_sums = state8[...].T
    tails[...] = jnp.zeros_like(tails)
    spare = jnp.zeros((4, 8, 128), F32)
    qx[20:24] = spare
    qy[5:8] = spare[0:3]
    qz[5:8] = spare[0:3]
    grad[0, 158:160] = spare[0:2]
    grad[1, 158:160] = spare[0:2]
    loads[6].wait()
    ops_split = [split(ops[r]) for r in range(2)]
    ops_t = [split(ops[r].T) for r in range(2)]

    for entry in relays:
        relay(*entry)

    in_high, in_low = [], []
    for p, part in enumerate(parts):
        got_l[2 * p].wait_recv()
        got_l[2 * p + 1].wait_recv()
        high, low = split(left[0, part, :])
        in_high.append(dot(high, hot_src_t).astype(BF16))
        in_low.append(dot(low, hot_src_t).astype(BF16))
    inputs = (jnp.concatenate(in_high, axis=0), jnp.concatenate(in_low, axis=0))
    mapped = jnp.where(rel < 0.5, dot3(ops_t[0], inputs), dot3(ops_t[1], inputs))
    inv_mapped = lax.rsqrt(jnp.sum(mapped * mapped, 0, keepdims=True) + 1e-06)
    unit_mapped = mapped * inv_mapped
    unit_rows = [split(unit_mapped[0:CUT].T), split(unit_mapped[CUT:WIDTH].T)]

    scores, square, right_split = 0.0, 0.0, []
    for p, part in enumerate(parts):
        got_r[2 * p].wait_recv()
        got_r[2 * p + 1].wait_recv()
        value = right[0, part, :]
        square = square + jnp.sum(value * value, 0, keepdims=True)
        right_split.append(split(value))
        scores = scores + dot3(unit_rows[p], right_split[p])
    inv_right = lax.rsqrt(square + 1e-06)
    scores = scores * inv_right
    positive = jnp.exp(jnp.sum(hot_tgt * scores, -1, keepdims=True))
    weights = multiplicity * jnp.exp(scores)
    norm = positive + jnp.sum(weights, -1, keepdims=True)
    scale = live / norm
    pull = weights * scale + hot_tgt * (positive * scale - live)
    pull_split = split(pull * inv_right)
    d_unit = jnp.concatenate([dot3(right_split[p], pull_split, NT) for p in range(2)], axis=0)
    d_mapped = inv_mapped * (d_unit - unit_mapped * jnp.sum(unit_mapped * d_unit, 0, keepdims=True))

    def operator_grad(kind, slot):
        high, low = split(jnp.where(rel == kind.astype(F32), d_mapped, 0.0))
        main = dot3(inputs, (high[0:ROWS], low[0:ROWS]), NT)
        for j in range(3):
            grad[slot, 50 * j:50 * j + 50] = main[:, 128 * j:128 * j + 128].reshape(50, 8, 128)
        tails[:, 0:WIDTH] = dot3((high[ROWS:WIDTH], low[ROWS:WIDTH]), inputs, NT)
        for i in range(2):
            for j in range(4):
                grad[slot, 150 + 4 * i + j] = tails[8 * i:8 * i + 8, 128 * j:128 * j + 128]

    operator_grad(other, 0)
    first = (("x", X0, XC, rx, 0), ("y", Y0, YC, ry, 3), ("z", Z0, ZC, rz, 10))
    pair_copies = []
    for part, (axis, start, count, _, _) in enumerate(first):
        span = pl.ds(start, count * size[axis])
        pair_copies.append(send(grad.at[0, span], sibling.at[span], core_send.at[part], core_recv.at[part], pair))
    operator_grad(mc, 1)
    copies1 = []
    for part, (axis, start, count, slots, base) in enumerate(first):
        pair_copies[part].wait_recv()
        span = pl.ds(start, count * size[axis])
        total[span] = grad[1, span] + sibling[span]
        for steps in range(1, size[axis]):
            to = (me[axis] + steps) % size[axis]
            k = base + steps - 1
            chunk = total.at[pl.ds(start + to * count, count)]
            copies1.append(send(chunk, slots.at[steps - 1], s1.at[k], v1.at[k], along(axis, steps)))

    rstate_copy.wait_recv()
    lstate_copy.wait_recv()
    unit_right = right[0] * inv_right
    d_right_unit = dot3(split(unit_mapped), split(pull))
    d_right = inv_right * (
        d_right_unit - unit_right * jnp.sum(unit_right * d_right_unit, 0, keepdims=True)
    )
    out_right[...] = adagrad(right[0], rstate[...], d_right, 0)
    right_out = pltpu.make_async_copy(out_right, new_right_ref, out_sem.at[0])
    right_out.start()
    d_inputs = dot3(ops_split[0], split(jnp.where(rel < 0.5, d_mapped, 0.0))) + dot3(
        ops_split[1], split(jnp.where(rel < 0.5, 0.0, d_mapped))
    )
    d_high, d_low = split(d_inputs)
    d_left = dot(d_high, hot_src) + dot(d_low, hot_src)
    out_left[...] = adagrad(left[0], lstate[...], d_left, 0)
    left_out = pltpu.make_async_copy(out_left, new_left_ref, out_sem.at[1])
    left_out.start()

    second = (("y", qx, r2x, 0, 3), ("z", qy, r2y, 7, 1), ("y", qz, r2z, 14, 1))
    copies2 = []
    for part, (axis1, start, count, slots, base1) in enumerate(first):
        axis, pieces, slots2, base, many = second[part]
        for steps in range(1, size[axis1]):
            copies1[base1 + steps - 1].wait_recv()
        value = total[pl.ds(start + me[axis1] * count, count)]
        for slot in range(size[axis1] - 1):
            value = value + slots[slot]
        pieces[0:count] = value
        for steps in range(1, size[axis]):
            to = (me[axis] + steps) % size[axis]
            k = base + steps - 1
            piece = pieces.at[pl.ds(to * many, many)]
            copies2.append(send(piece, slots2.at[steps - 1], s2.at[k], v2.at[k], along(axis, steps)))

    third = (("z", r3x, 0), ("x", r3y, 7), ("x", r3z, 10))
    copies3 = []
    for part, (axis2, pieces, slots2, base2, many) in enumerate(second):
        axis, slots, base = third[part]
        for steps in range(1, size[axis2]):
            copies2[base2 + steps - 1].wait_recv()
        value = pieces[pl.ds(me[axis2] * many, many)]
        for slot in range(size[axis2] - 1):
            value = value + slots2[slot]
        slots[me[axis]] = value
        for steps in range(1, size[axis]):
            k = base + steps - 1
            slot = slots.at[me[axis]]
            copies3.append(send(slot, slot, s3.at[k], v3.at[k], along(axis, steps)))

    finals = (fx, fy, fz)
    copies4 = []
    for part, (axis3, slots, base3) in enumerate(third):
        axis1 = first[part][0]
        axis2, _, _, base, many = second[part]
        for steps in range(1, size[axis3]):
            copies3[base3 + steps - 1].wait_recv()
        value = slots[0]
        for slot in range(1, size[axis3]):
            value = value + slots[slot]
        place = pl.ds(me[axis2] * many, many)
        finals[part][mc, me[axis1], place] = value
        piece = finals[part].at[mc, me[axis1], place]
        for steps in range(1, size[axis2]):
            k = base + steps - 1
            copies4.append(send(piece, piece, s4.at[k], v4.at[k], along(axis2, steps)))

    copies5, copies6 = [], []
    for part, (axis1, _, count, _, base1) in enumerate(first):
        axis2, _, _, base2, _ = second[part]
        for steps in range(1, size[axis2]):
            copies4[base2 + steps - 1].wait_recv()
        chunk = finals[part].at[mc, me[axis1], pl.ds(0, count)]
        for steps in range(1, size[axis1]):
            k = base1 + steps - 1
            copies5.append(send(chunk, chunk, s5.at[k], v5.at[k], along(axis1, steps)))
        copies6.append(send(chunk, chunk, s6.at[part], v6.at[part], pair))
    for part, (axis1, _, count, _, base1) in enumerate(first):
        for steps in range(1, size[axis1]):
            k = base1 + steps - 1
            copies5[k].wait_recv()
            chunk = finals[part].at[mc, (me[axis1] + size[axis1] - steps) % size[axis1], pl.ds(0, count)]
            copies6.append(send(chunk, chunk, s6.at[3 + k], v6.at[3 + k], pair))
    ops_out = []
    for turn, kind in enumerate((mc, other)):
        if turn:
            for copy in copies6:
                copy.wait_recv()
        for part, (axis1, start, count, _, _) in enumerate(first):
            for j in range(size[axis1]):
                for i in range(count):
                    unit = start + j * count + i
                    if unit < 150:
                        row, column = 8 * (unit % 50), 128 * (unit // 50)
                        gsum[row:row + 8, column:column + 128] = finals[part][kind, j, i]
                    elif unit < 158:
                        row, column = 8 * ((unit - 150) // 4), 128 * ((unit - 150) % 4)
                        tails[row:row + 8, column:column + 128] = finals[part][kind, j, i]
        gsum[:, ROWS:WIDTH] = tails[...].T[0:WIDTH]
        sums = jnp.where(kind == 0, op_sums[0:WIDTH, 0:1], op_sums[0:WIDTH, 1:2])
        out_ops[kind] = adagrad(ops[kind], sums, gsum[...], 1)
        ops_out.append(pltpu.make_async_copy(out_ops.at[kind], new_ops_ref.at[kind], out_sem.at[2 + turn]))
        ops_out[turn].start()
    for here, buffer, p, base, _ in relays:
        relayed(here, buffer, p, base)
    for copy in sent + pair_copies + copies1 + copies2 + copies3 + copies4 + copies5 + copies6:
        copy.wait_send()
    right_out.wait()
    left_out.wait()
    ops_out[0].wait()
    ops_out[1].wait()


def hand_over(left_ref, right_ref, ops_ref, new_left_ref, new_right_ref, new_ops_ref, blocks, ops, sems):
    steps = []
    for i, (source, target) in enumerate(((left_ref, new_left_ref), (right_ref, new_right_ref))):
        for start in range(0, WIDTH, 200):
            part = pl.ds(start, 200)
            steps.append((source.at[part], blocks.at[i, part], target.at[part]))
    for kind in range(2):
        for start in range(0, WIDTH, 200):
            part = pl.ds(start, 200)
            steps.append((ops_ref.at[kind, part], ops.at[kind, part], new_ops_ref.at[kind, part]))
    loads = [pltpu.make_async_copy(a, b, sems.at[0, i]) for i, (a, b, _) in enumerate(steps)]
    stores = [pltpu.make_async_copy(b, c, sems.at[1, i]) for i, (_, b, c) in enumerate(steps)]
    for load in loads:
        load.start()
    for load, store in zip(loads, stores):
        load.wait()
        store.start()
    for store in stores:
        store.wait()


def body(
    left_table, left_state, right_table, right_state, operators, operator_state,
    sources, targets, relations, negatives, counts,
):
    hbm = pl.BlockSpec(memory_space=pl.ANY)
    dma = pltpu.SemaphoreType.DMA

    def buf(*shape):
        return pltpu.VMEM(shape, F32)

    def units(*shape):
        return pltpu.VMEM(shape + (8, 128), F32)

    block = jax.ShapeDtypeStruct((WIDTH, ROWS), F32)
    results = (block, block, jax.ShapeDtypeStruct((2, WIDTH, WIDTH), F32))
    trained = pl.pallas_call(
        kernel,
        out_shape=results,
        in_specs=[hbm] * 11,
        out_specs=(hbm, hbm, hbm),
        scratch_shapes=[
            buf(2, WIDTH, ROWS), buf(2, WIDTH, ROWS), buf(1, ROWS), buf(1, ROWS), buf(2, WIDTH, WIDTH),
            buf(WIDTH, ROWS), buf(WIDTH, ROWS), buf(2, WIDTH, WIDTH), buf(8, ROWS), buf(8, 512),
            buf(16, 512), buf(WIDTH, WIDTH),
            units(2, UNITS), units(UNITS), units(UNITS),
            units(3, XC), units(7, YC), units(7, ZC),
            units(24), units(8), units(8),
            units(7, 3), units(7, 1), units(7, 1),
            units(8, 3), units(4, 1), units(4, 1),
            units(2, 4, 24), units(2, 8, 8), units(2, 8, 8),
            buf(2, WIDTH), *[pltpu.VMEM((1, ROWS), jnp.int32)] * 4, pltpu.VMEM((1, 1), jnp.int32),
            dma((18,)), dma((2, 10)), dma((7,)), dma((4,)),
            dma((3,)), dma((3,)), dma((17,)), dma((17,)), dma((21,)), dma((21,)),
            dma((13,)), dma((13,)), dma((21,)), dma((21,)), dma((17,)), dma((17,)),
            dma((20,)), dma((20,)),
        ],
        compiler_params=pltpu.CompilerParams(
            collective_id=0, has_side_effects=True, vmem_limit_bytes=VMEM_BYTES
        ),
        name="bucket_round",
    )(
        left_table.reshape(ROWS, WIDTH).T, left_state.reshape(1, ROWS),
        right_table.reshape(ROWS, WIDTH).T, right_state.reshape(1, ROWS),
        operators, operator_state,
        sources.reshape(1, ROWS), targets.reshape(1, ROWS),
        relations.reshape(1, ROWS), negatives.reshape(1, ROWS), counts,
    )
    new_left, new_right, new_operators = pl.pallas_call(
        hand_over,
        out_shape=results,
        in_specs=[hbm] * 3,
        out_specs=(hbm, hbm, hbm),
        scratch_shapes=[buf(2, WIDTH, ROWS), buf(2, WIDTH, WIDTH), dma((2, 8))],
        compiler_params=pltpu.CompilerParams(vmem_limit_bytes=VMEM_BYTES),
        name="hand_over",
    )(*trained)
    return new_left.T[None, None], new_right.T[None, None], new_operators


def solution(mesh):
    edges = P("lhs", "rhs", None)
    blocks = P("lhs", "rhs", None, None)
    return jax.shard_map(
        body,
        mesh=mesh,
        in_specs=(blocks, edges, blocks, edges, P(), P(), edges, edges, edges, edges, P("lhs", "rhs")),
        out_specs=(blocks, blocks, P()),
        check_vma=False,
    )
```

```python
import functools

import jax
import jax.numpy as jnp
from jax import lax
from jax.experimental import pallas as pl
from jax.experimental.pallas import tpu as pltpu
from jax.sharding import PartitionSpec as P

MESH = pl.DeviceIdType.MESH
F32 = jnp.float32
BF16 = jnp.bfloat16

ROWS = 384
WIDTH = 400
VMEM_BYTES = 64 * 2**20 - 4096
NX, NY, NZ = 4, 8, 8
CUT = 208
PIECES = ((0, 104), (104, 104), (208, 96), (304, 96))

UNITS = 160
XC, YC, ZC = 16, 6, 6
X0, Y0, Z0 = 0, 64, 112

NN = (((1,), (0,)), ((), ()))
NT = (((1,), (1,)), ((), ()))


def split(value):
    high = value.astype(BF16)
    return high, (value - high.astype(F32)).astype(BF16)


def dot(a, b, dims=NN):
    return lax.dot_general(a, b, dims, preferred_element_type=F32)


def dot3(a, b, dims=NN):
    (a_high, a_low), (b_high, b_low) = a, b
    return dot(a_high, b_high, dims) + (dot(a_high, b_low, dims) + dot(a_low, b_high, dims))


def device(x, y, z, c):
    return ((z // 4) * 16 + y * 2 + c, (z % 4) * 4 + x)


def adagrad(weights, sums, gradient, axis):
    summed = sums + jnp.sum(gradient * gradient, axis, keepdims=True) * (1.0 / WIDTH)
    return weights - gradient * (0.1 / jnp.sqrt(summed))


def kernel(
    left_ref, lstate_ref, right_ref, rstate_ref, ops_ref, opstate_hbm,
    src_hbm, tgt_hbm, rel_hbm, neg_hbm, cnt_hbm,
    new_left_ref, new_right_ref, new_ops_ref,
    left, right, lstate, rstate, ops, out_left, out_right, out_ops, rows8, state8, tails, gsum,
    grad, sibling, total,
    rx, ry, rz, qx, qy, qz, r2x, r2y, r2z, r3x, r3y, r3z, fx, fy, fz,
    opstate_ref, src_ref, tgt_ref, rel_ref, neg_ref, cnt_ref,
    perm_send, perm_recv, local_sem, out_sem,
    core_send, core_recv, s1, v1, s2, v2, s3, v3, s4, v4, s5, v5, s6, v6,
):
    lhs, rhs = lax.axis_index("lhs"), lax.axis_index("rhs")
    mx, my, mz, mc = rhs % 4, (lhs // 2) % 8, (lhs // 16) * 4 + rhs // 4, lhs % 2
    other = 1 - mc

    def along(axis, steps):
        if axis == "x":
            return device((mx + steps) % NX, my, mz, mc)
        if axis == "y":
            return device(mx, (my + steps) % NY, mz, mc)
        return device(mx, my, (mz + steps) % NZ, mc)

    pair = device(mx, my, mz, other)
    size = {"x": NX, "y": NY, "z": NZ}
    me = {"x": mx, "y": my, "z": mz}

    def far(axis):
        return sorted(range(1, size[axis]), key=lambda d: -min(d, size[axis] - d))

    peers = [((lhs + 1) % 32, rhs), ((lhs + 31) % 32, rhs), (lhs, (rhs + 1) % 16), (lhs, (rhs + 15) % 16)]
    peers += [pair, (lhs + 15 - 2 * (lhs % 16), rhs)]
    peers += [along(axis, steps) for axis in "xyz" for steps in range(1, size[axis])]
    barrier = pltpu.get_barrier_semaphore()
    for peer in peers:
        pl.semaphore_signal(barrier, inc=1, device_id=peer, device_id_type=MESH)
    place = lhs % 16
    for spot, steps in ((15, (14, 3)), (13, (18, 19)), (2, (29, 30)), (0, (13, 2))):
        @pl.when(place == spot)
        def _():
            for step in steps:
                pl.semaphore_signal(
                    barrier, inc=1, device_id=((lhs + step) % 32, rhs), device_id_type=MESH
                )
    greeted = len(peers) + 2 * ((place == 15) | (place == 13) | (place == 2) | (place == 0)).astype(jnp.int32)
    loads = [
        pltpu.make_async_copy(far, near, local_sem.at[i])
        for i, (far, near) in enumerate((
            (src_hbm, src_ref), (tgt_hbm, tgt_ref), (rel_hbm, rel_ref), (neg_hbm, neg_ref), (cnt_hbm, cnt_ref),
            (opstate_hbm, opstate_ref), (ops_ref, ops),
        ))
    ]
    for load in loads:
        load.start()
    pl.semaphore_wait(barrier, greeted)

    def make(src, dst, ssem, rsem, target):
        return pltpu.make_async_remote_copy(
            src_ref=src, dst_ref=dst, send_sem=ssem, recv_sem=rsem, device_id=target, device_id_type=MESH
        )

    def send(src, dst, ssem, rsem, target):
        copy = make(src, dst, ssem, rsem, target)
        copy.start()
        return copy

    parts = (pl.ds(0, CUT), pl.ds(CUT, WIDTH - CUT))
    corner_r, corner_l = (rhs % 4) == 3, (lhs % 16) == 15
    next_r, next_l = (rhs + 1) % 16, (lhs + 1) % 32
    hop_r = (jnp.where(corner_r, rhs - 3, next_r),) * 2 + (jnp.where(corner_r, (rhs + 4) % 16, next_r),) * 2
    hop_l = (
        next_l,
        jnp.where(corner_l, (lhs + 16) % 32, next_l),
        jnp.where(corner_l, (lhs + 14) % 32, next_l),
        jnp.where(corner_l, (lhs + 3) % 32, next_l),
    )
    slot_r = (corner_r.astype(jnp.int32),) * 4
    slot_l = (0,) + (corner_l.astype(jnp.int32),) * 3
    sent, got_r, got_l = [], {}, {}
    for p in (0, 2, 1, 3):
        part = pl.ds(*PIECES[p])
        sent.append(send(
            left_ref.at[part], left.at[slot_l[p], part],
            perm_send.at[4 + p], perm_recv.at[slot_l[p], 4 + p], (hop_l[p], rhs),
        ))
        sent.append(send(
            right_ref.at[part], right.at[slot_r[p], part],
            perm_send.at[p], perm_recv.at[slot_r[p], p], (lhs, hop_r[p]),
        ))
        got_r[p] = make(right.at[1, part], right.at[0, part], perm_send.at[10 + p], perm_recv.at[0, p], pair)
        got_l[p] = make(left.at[1, part], left.at[0, part], perm_send.at[14 + p], perm_recv.at[0, 4 + p], pair)
    rstate_copy = send(rstate_ref, rstate, perm_send.at[8], perm_recv.at[0, 8], (lhs, next_r))
    lstate_copy = send(lstate_ref, lstate, perm_send.at[9], perm_recv.at[0, 9], (next_l, rhs))
    sent += [rstate_copy, lstate_copy]

    def relay(here, buffer, p, base, target):
        part, sem = pl.ds(*PIECES[p]), perm_send.at[10 + base + p]

        @pl.when(here)
        def _():
            make(buffer.at[0, part], buffer.at[1, part], sem, perm_recv.at[1, base + p], pair).wait_recv()
            make(buffer.at[1, part], buffer.at[0, part], sem, perm_recv.at[0, base + p], target).start()

    def relayed(here, buffer, p, base):
        part, sem = pl.ds(*PIECES[p]), perm_send.at[10 + base + p]

        @pl.when(here)
        def _():
            make(buffer.at[1, part], buffer.at[0, part], sem, perm_recv.at[0, base + p], pair).wait_send()

    relays = [
        (corner_r, right, 2, 0, (lhs, rhs - 3)),
        ((rhs % 4) == 0, right, 0, 0, (lhs, (rhs + 4) % 16)),
        (corner_l, left, 1, 4, (lhs - 15, rhs)),
        ((lhs % 16) == 13, left, 2, 4, (lhs - 13, rhs)),
        ((lhs % 16) == 2, left, 3, 4, (lhs - 2, rhs)),
        (corner_r, right, 3, 0, (lhs, rhs - 3)),
        ((rhs % 4) == 0, right, 1, 0, (lhs, (rhs + 4) % 16)),
    ]

    for load in loads[:6]:
        load.wait()
    rows8[0:1, :] = src_ref[...].astype(F32)
    rows8[1:2, :] = tgt_ref[...].astype(F32)
    rows8[2:3, :] = rel_ref[...].astype(F32)
    rows8[3:4, :] = neg_ref[...].astype(F32)
    rows8[4:8, :] = jnp.zeros((4, ROWS), F32)
    columns = rows8[...].T
    lane = lax.broadcasted_iota(jnp.int32, (ROWS, ROWS), 1).astype(F32)
    sublane = lax.broadcasted_iota(jnp.int32, (ROWS, ROWS), 0).astype(F32)
    hot_src = (columns[:, 0:1] == lane).astype(F32).astype(BF16)
    hot_src_t = (rows8[0:1, :] == sublane).astype(F32).astype(BF16)
    hot_tgt = (columns[:, 1:2] == lane).astype(F32)
    hot_neg = (columns[:, 3:4] == lane).astype(F32)
    multiplicity = jnp.sum(hot_neg, axis=0, keepdims=True)
    rel = rows8[2:3, :]
    edge = lax.broadcasted_iota(jnp.int32, (ROWS, 1), 0)
    live = (edge < cnt_ref[...]).astype(F32)
    state8[...] = jnp.zeros_like(state8)
    state8[0:2, 0:WIDTH] = opstate_ref[...]
    op_sums = state8[...].T
    tails[...] = jnp.zeros_like(tails)
    spare = jnp.zeros((4, 8, 128), F32)
    qy[6:8] = spare[0:2]
    qz[6:8] = spare[0:2]
    grad[0, 158:160] = spare[0:2]
    grad[1, 158:160] = spare[0:2]
    loads[6].wait()
    ops_split = [split(ops[r]) for r in range(2)]
    ops_t = [split(ops[r].T) for r in range(2)]

    for entry in relays:
        relay(*entry)

    in_high, in_low = [], []
    for p, part in enumerate(parts):
        got_l[2 * p].wait_recv()
        got_l[2 * p + 1].wait_recv()
        high, low = split(left[0, part, :])
        in_high.append(dot(high, hot_src_t).astype(BF16))
        in_low.append(dot(low, hot_src_t).astype(BF16))
    inputs = (jnp.concatenate(in_high, axis=0), jnp.concatenate(in_low, axis=0))
    mapped = jnp.where(rel < 0.5, dot3(ops_t[0], inputs), dot3(ops_t[1], inputs))
    inv_mapped = lax.rsqrt(jnp.sum(mapped * mapped, 0, keepdims=True) + 1e-06)
    unit_mapped = mapped * inv_mapped
    unit_rows = [split(unit_mapped[0:CUT].T), split(unit_mapped[CUT:WIDTH].T)]

    scores, square, right_split = 0.0, 0.0, []
    for p, part in enumerate(parts):
        got_r[2 * p].wait_recv()
        got_r[2 * p + 1].wait_recv()
        value = right[0, part, :]
        square = square + jnp.sum(value * value, 0, keepdims=True)
        right_split.append(split(value))
        scores = scores + dot3(unit_rows[p], right_split[p])
    inv_right = lax.rsqrt(square + 1e-06)
    scores = scores * inv_right
    positive = jnp.exp(jnp.sum(hot_tgt * scores, -1, keepdims=True))
    weights = multiplicity * jnp.exp(scores)
    norm = positive + jnp.sum(weights, -1, keepdims=True)
    scale = live / norm
    pull = weights * scale + hot_tgt * (positive * scale - live)
    pull_split = split(pull * inv_right)
    d_unit = jnp.concatenate([dot3(right_split[p], pull_split, NT) for p in range(2)], axis=0)
    d_mapped = inv_mapped * (d_unit - unit_mapped * jnp.sum(unit_mapped * d_unit, 0, keepdims=True))

    def operator_grad(kind, slot):
        high, low = split(jnp.where(rel == kind.astype(F32), d_mapped, 0.0))
        main = dot3(inputs, (high[0:ROWS], low[0:ROWS]), NT)
        for j in range(3):
            grad[slot, 50 * j:50 * j + 50] = main[:, 128 * j:128 * j + 128].reshape(50, 8, 128)
        tails[:, 0:WIDTH] = dot3((high[ROWS:WIDTH], low[ROWS:WIDTH]), inputs, NT)
        for i in range(2):
            for j in range(4):
                grad[slot, 150 + 4 * i + j] = tails[8 * i:8 * i + 8, 128 * j:128 * j + 128]

    operator_grad(other, 0)
    first = (("x", X0, XC, rx, 0), ("y", Y0, YC, ry, 3), ("z", Z0, ZC, rz, 10))
    pair_copies = []
    for part, (axis, start, count, _, _) in enumerate(first):
        span = pl.ds(start, count * size[axis])
        pair_copies.append(send(grad.at[0, span], sibling.at[span], core_send.at[part], core_recv.at[part], pair))
    operator_grad(mc, 1)
    copies1 = {}
    for part, (axis, start, count, slots, base) in enumerate(first):
        pair_copies[part].wait_recv()
        span = pl.ds(start, count * size[axis])
        total[span] = grad[1, span] + sibling[span]
        for steps in far(axis):
            to = (me[axis] + steps) % size[axis]
            k = base + steps - 1
            chunk = total.at[pl.ds(start + to * count, count)]
            copies1[k] = send(chunk, slots.at[steps - 1], s1.at[k], v1.at[k], along(axis, steps))

    rstate_copy.wait_recv()
    lstate_copy.wait_recv()
    unit_right = right[0] * inv_right
    d_right_unit = dot3(split(unit_mapped), split(pull))
    d_right = inv_right * (
        d_right_unit - unit_right * jnp.sum(unit_right * d_right_unit, 0, keepdims=True)
    )
    out_right[...] = adagrad(right[0], rstate[...], d_right, 0)
    right_out = pltpu.make_async_copy(out_right, new_right_ref, out_sem.at[0])
    right_out.start()
    d_inputs = dot3(ops_split[0], split(jnp.where(rel < 0.5, d_mapped, 0.0))) + dot3(
        ops_split[1], split(jnp.where(rel < 0.5, 0.0, d_mapped))
    )
    d_high, d_low = split(d_inputs)
    d_left = dot(d_high, hot_src) + dot(d_low, hot_src)
    out_left[...] = adagrad(left[0], lstate[...], d_left, 0)
    left_out = pltpu.make_async_copy(out_left, new_left_ref, out_sem.at[1])
    left_out.start()

    second = (("y", qx, r2x, 0, 2), ("x", qy, r2y, 7, 2), ("x", qz, r2z, 10, 2))
    copies2, copies3, copies4, copies5, copies6 = {}, {}, {}, {}, {}
    for part, (axis1, start, count, slots, base1) in enumerate(first):
        axis, pieces, slots2, base, many = second[part]
        for steps in range(1, size[axis1]):
            copies1[base1 + steps - 1].wait_recv()
        value = total[pl.ds(start + me[axis1] * count, count)]
        for slot in range(size[axis1] - 1):
            value = value + slots[slot]
        pieces[0:count] = value
        for steps in far(axis):
            to = (me[axis] + steps) % size[axis]
            k = base + steps - 1
            piece = pieces.at[pl.ds(to * many, many)]
            copies2[k] = send(piece, slots2.at[steps - 1], s2.at[k], v2.at[k], along(axis, steps))

    third = (("z", r3x, 0), ("z", r3y, 7), ("y", r3z, 14))
    for part in (0, 1, 2):
        axis2, pieces, slots2, base2, many = second[part]
        axis, slots, base = third[part]
        for steps in range(1, size[axis2]):
            copies2[base2 + steps - 1].wait_recv()
        value = pieces[pl.ds(me[axis2] * many, many)]
        for slot in range(size[axis2] - 1):
            value = value + slots2[slot]
        slots[me[axis]] = value
        for steps in far(axis):
            k = base + steps - 1
            slot = slots.at[me[axis]]
            copies3[k] = send(slot, slot, s3.at[k], v3.at[k], along(axis, steps))

    finals = (fx, fy, fz)
    for part in (0, 1, 2):
        axis3, slots, base3 = third[part]
        axis1 = first[part][0]
        axis2, _, _, base, many = second[part]
        for steps in range(1, size[axis3]):
            copies3[base3 + steps - 1].wait_recv()
        value = slots[0]
        for slot in range(1, size[axis3]):
            value = value + slots[slot]
        place = pl.ds(me[axis2] * many, many)
        finals[part][mc, me[axis1], place] = value
        piece = finals[part].at[mc, me[axis1], place]
        for steps in far(axis2):
            k = base + steps - 1
            copies4[k] = send(piece, piece, s4.at[k], v4.at[k], along(axis2, steps))

    for part in (0, 1, 2):
        axis1, _, count, _, base1 = first[part]
        axis2, _, _, base2, _ = second[part]
        for steps in range(1, size[axis2]):
            copies4[base2 + steps - 1].wait_recv()
        chunk = finals[part].at[mc, me[axis1], pl.ds(0, count)]
        for steps in far(axis1):
            k = base1 + steps - 1
            copies5[k] = send(chunk, chunk, s5.at[k], v5.at[k], along(axis1, steps))
        copies6[part] = send(chunk, chunk, s6.at[part], v6.at[part], pair)
    for part, (axis1, _, count, _, base1) in enumerate(first):
        for steps in sorted(range(1, size[axis1]), key=lambda d: min(d, size[axis1] - d)):
            k = base1 + steps - 1
            copies5[k].wait_recv()
            chunk = finals[part].at[mc, (me[axis1] + size[axis1] - steps) % size[axis1], pl.ds(0, count)]
            copies6[3 + k] = send(chunk, chunk, s6.at[3 + k], v6.at[3 + k], pair)
    ops_out = []
    for turn, kind in enumerate((mc, other)):
        if turn:
            for copy in copies6.values():
                copy.wait_recv()
        for part, (axis1, start, count, _, _) in enumerate(first):
            for j in range(size[axis1]):
                for i in range(count):
                    unit = start + j * count + i
                    if unit < 150:
                        row, column = 8 * (unit % 50), 128 * (unit // 50)
                        gsum[row:row + 8, column:column + 128] = finals[part][kind, j, i]
                    elif unit < 158:
                        row, column = 8 * ((unit - 150) // 4), 128 * ((unit - 150) % 4)
                        tails[row:row + 8, column:column + 128] = finals[part][kind, j, i]
        gsum[:, ROWS:WIDTH] = tails[...].T[0:WIDTH]
        sums = jnp.where(kind == 0, op_sums[0:WIDTH, 0:1], op_sums[0:WIDTH, 1:2])
        out_ops[kind] = adagrad(ops[kind], sums, gsum[...], 1)
        ops_out.append(pltpu.make_async_copy(out_ops.at[kind], new_ops_ref.at[kind], out_sem.at[2 + turn]))
        ops_out[turn].start()
    for here, buffer, p, base, _ in relays:
        relayed(here, buffer, p, base)
    for copy in sent + pair_copies:
        copy.wait_send()
    for copies in (copies1, copies2, copies3, copies4, copies5, copies6):
        for copy in copies.values():
            copy.wait_send()
    right_out.wait()
    left_out.wait()
    ops_out[0].wait()
    ops_out[1].wait()


def hand_over(left_ref, right_ref, ops_ref, new_left_ref, new_right_ref, new_ops_ref, blocks, ops, sems):
    steps = []
    for i, (source, target) in enumerate(((left_ref, new_left_ref), (right_ref, new_right_ref))):
        for start in range(0, WIDTH, 200):
            part = pl.ds(start, 200)
            steps.append((source.at[part], blocks.at[i, part], target.at[part]))
    for kind in range(2):
        for start in range(0, WIDTH, 200):
            part = pl.ds(start, 200)
            steps.append((ops_ref.at[kind, part], ops.at[kind, part], new_ops_ref.at[kind, part]))
    loads = [pltpu.make_async_copy(a, b, sems.at[0, i]) for i, (a, b, _) in enumerate(steps)]
    stores = [pltpu.make_async_copy(b, c, sems.at[1, i]) for i, (_, b, c) in enumerate(steps)]
    for load in loads:
        load.start()
    for load, store in zip(loads, stores):
        load.wait()
        store.start()
    for store in stores:
        store.wait()


def body(
    left_table, left_state, right_table, right_state, operators, operator_state,
    sources, targets, relations, negatives, counts,
):
    hbm = pl.BlockSpec(memory_space=pl.ANY)
    dma = pltpu.SemaphoreType.DMA

    def buf(*shape):
        return pltpu.VMEM(shape, F32)

    def units(*shape):
        return pltpu.VMEM(shape + (8, 128), F32)

    block = jax.ShapeDtypeStruct((WIDTH, ROWS), F32)
    results = (block, block, jax.ShapeDtypeStruct((2, WIDTH, WIDTH), F32))
    trained = pl.pallas_call(
        kernel,
        out_shape=results,
        in_specs=[hbm] * 11,
        out_specs=(hbm, hbm, hbm),
        scratch_shapes=[
            buf(2, WIDTH, ROWS), buf(2, WIDTH, ROWS), buf(1, ROWS), buf(1, ROWS), buf(2, WIDTH, WIDTH),
            buf(WIDTH, ROWS), buf(WIDTH, ROWS), buf(2, WIDTH, WIDTH), buf(8, ROWS), buf(8, 512),
            buf(16, 512), buf(WIDTH, WIDTH),
            units(2, UNITS), units(UNITS), units(UNITS),
            units(3, XC), units(7, YC), units(7, ZC),
            units(XC), units(8), units(8),
            units(7, 2), units(3, 2), units(3, 2),
            units(8, 2), units(8, 2), units(8, 2),
            units(2, 4, XC), units(2, 8, 8), units(2, 8, 8),
            buf(2, WIDTH), *[pltpu.VMEM((1, ROWS), jnp.int32)] * 4, pltpu.VMEM((1, 1), jnp.int32),
            dma((18,)), dma((2, 10)), dma((7,)), dma((4,)),
            dma((3,)), dma((3,)), dma((17,)), dma((17,)), dma((13,)), dma((13,)),
            dma((21,)), dma((21,)), dma((13,)), dma((13,)), dma((17,)), dma((17,)),
            dma((20,)), dma((20,)),
        ],
        compiler_params=pltpu.CompilerParams(
            collective_id=0, has_side_effects=True, vmem_limit_bytes=VMEM_BYTES
        ),
        name="bucket_round",
    )(
        left_table.reshape(ROWS, WIDTH).T, left_state.reshape(1, ROWS),
        right_table.reshape(ROWS, WIDTH).T, right_state.reshape(1, ROWS),
        operators, operator_state,
        sources.reshape(1, ROWS), targets.reshape(1, ROWS),
        relations.reshape(1, ROWS), negatives.reshape(1, ROWS), counts,
    )
    new_left, new_right, new_operators = pl.pallas_call(
        hand_over,
        out_shape=results,
        in_specs=[hbm] * 3,
        out_specs=(hbm, hbm, hbm),
        scratch_shapes=[buf(2, WIDTH, ROWS), buf(2, WIDTH, WIDTH), dma((2, 8))],
        compiler_params=pltpu.CompilerParams(vmem_limit_bytes=VMEM_BYTES),
        name="hand_over",
    )(*trained)
    return new_left.T[None, None], new_right.T[None, None], new_operators


def solution(mesh):
    edges = P("lhs", "rhs", None)
    blocks = P("lhs", "rhs", None, None)
    return jax.shard_map(
        body,
        mesh=mesh,
        in_specs=(blocks, edges, blocks, edges, P(), P(), edges, edges, edges, edges, P("lhs", "rhs")),
        out_specs=(blocks, blocks, P()),
        check_vma=False,
    )
```

```python
import functools

import jax
import jax.numpy as jnp
from jax import lax
from jax.experimental import pallas as pl
from jax.experimental.pallas import tpu as pltpu
from jax.sharding import PartitionSpec as P

MESH = pl.DeviceIdType.MESH
F32 = jnp.float32
BF16 = jnp.bfloat16

ROWS = 384
WIDTH = 400
VMEM_BYTES = 64 * 2**20 - 4096
NX, NY, NZ = 4, 8, 8
CUT = 208
PIECES = ((0, 104), (104, 104), (208, 96), (304, 96))

UNITS = 160
XC, YC, ZC = 16, 6, 6
X0, Y0, Z0 = 0, 64, 112

NN = (((1,), (0,)), ((), ()))
NT = (((1,), (1,)), ((), ()))


def split(value):
    high = value.astype(BF16)
    return high, (value - high.astype(F32)).astype(BF16)


def dot(a, b, dims=NN):
    return lax.dot_general(a, b, dims, preferred_element_type=F32)


def dot3(a, b, dims=NN):
    (a_high, a_low), (b_high, b_low) = a, b
    return dot(a_high, b_high, dims) + (dot(a_high, b_low, dims) + dot(a_low, b_high, dims))


def device(x, y, z, c):
    return ((z // 4) * 16 + y * 2 + c, (z % 4) * 4 + x)


def adagrad(weights, sums, gradient, axis):
    summed = sums + jnp.sum(gradient * gradient, axis, keepdims=True) * (1.0 / WIDTH)
    return weights - gradient * (0.1 / jnp.sqrt(summed))


def kernel(
    left_ref, lstate_ref, right_ref, rstate_ref, ops_ref, opstate_hbm,
    src_hbm, tgt_hbm, rel_hbm, neg_hbm, cnt_hbm,
    new_left_ref, new_right_ref, new_ops_ref,
    left, right, lstate, rstate, ops, out_left, out_right, out_ops, rows8, state8, tails, gsum,
    grad, sibling, total,
    rx, ry, rz, qx, qy, qz, r2x, r2y, r2z, r3x, r3y, r3z, fx, fy, fz,
    opstate_ref, src_ref, tgt_ref, rel_ref, neg_ref, cnt_ref,
    perm_send, perm_recv, local_sem, out_sem,
    core_send, core_recv, s1, v1, s2, v2, s3, v3, s4, v4, s5, v5, s6, v6,
):
    lhs, rhs = lax.axis_index("lhs"), lax.axis_index("rhs")
    mx, my, mz, mc = rhs % 4, (lhs // 2) % 8, (lhs // 16) * 4 + rhs // 4, lhs % 2
    other = 1 - mc

    def along(axis, steps):
        if axis == "x":
            return device((mx + steps) % NX, my, mz, mc)
        if axis == "y":
            return device(mx, (my + steps) % NY, mz, mc)
        return device(mx, my, (mz + steps) % NZ, mc)

    pair = device(mx, my, mz, other)
    size = {"x": NX, "y": NY, "z": NZ}
    me = {"x": mx, "y": my, "z": mz}

    def far(axis):
        return sorted(range(1, size[axis]), key=lambda d: -min(d, size[axis] - d))

    peers = [((lhs + 1) % 32, rhs), ((lhs + 31) % 32, rhs), (lhs, (rhs + 1) % 16), (lhs, (rhs + 15) % 16)]
    peers += [pair, (lhs + 15 - 2 * (lhs % 16), rhs)]
    peers += [along(axis, steps) for axis in "xyz" for steps in range(1, size[axis])]
    barrier = pltpu.get_barrier_semaphore()
    for peer in peers:
        pl.semaphore_signal(barrier, inc=1, device_id=peer, device_id_type=MESH)
    place = lhs % 16
    for spot, steps in ((15, (14, 3)), (13, (18, 19)), (2, (29, 30)), (0, (13, 2))):
        @pl.when(place == spot)
        def _():
            for step in steps:
                pl.semaphore_signal(
                    barrier, inc=1, device_id=((lhs + step) % 32, rhs), device_id_type=MESH
                )
    greeted = len(peers) + 2 * ((place == 15) | (place == 13) | (place == 2) | (place == 0)).astype(jnp.int32)
    loads = [
        pltpu.make_async_copy(far, near, local_sem.at[i])
        for i, (far, near) in enumerate((
            (src_hbm, src_ref), (tgt_hbm, tgt_ref), (rel_hbm, rel_ref), (neg_hbm, neg_ref), (cnt_hbm, cnt_ref),
            (opstate_hbm, opstate_ref), (ops_ref, ops),
        ))
    ]
    for load in loads:
        load.start()
    pl.semaphore_wait(barrier, greeted)

    def make(src, dst, ssem, rsem, target):
        return pltpu.make_async_remote_copy(
            src_ref=src, dst_ref=dst, send_sem=ssem, recv_sem=rsem, device_id=target, device_id_type=MESH
        )

    def send(src, dst, ssem, rsem, target):
        copy = make(src, dst, ssem, rsem, target)
        copy.start()
        return copy

    parts = (pl.ds(0, CUT), pl.ds(CUT, WIDTH - CUT))
    corner_r, corner_l = (rhs % 4) == 3, (lhs % 16) == 15
    next_r, next_l = (rhs + 1) % 16, (lhs + 1) % 32
    hop_r = (jnp.where(corner_r, rhs - 3, next_r),) * 2 + (jnp.where(corner_r, (rhs + 4) % 16, next_r),) * 2
    hop_l = (
        next_l,
        jnp.where(corner_l, (lhs + 16) % 32, next_l),
        jnp.where(corner_l, (lhs + 14) % 32, next_l),
        jnp.where(corner_l, (lhs + 3) % 32, next_l),
    )
    slot_r = (corner_r.astype(jnp.int32),) * 4
    slot_l = (0,) + (corner_l.astype(jnp.int32),) * 3
    sent, got_r, got_l = [], {}, {}
    for p in (0, 2, 1, 3):
        part = pl.ds(*PIECES[p])
        sent.append(send(
            left_ref.at[part], left.at[slot_l[p], part],
            perm_send.at[4 + p], perm_recv.at[slot_l[p], 4 + p], (hop_l[p], rhs),
        ))
        sent.append(send(
            right_ref.at[part], right.at[slot_r[p], part],
            perm_send.at[p], perm_recv.at[slot_r[p], p], (lhs, hop_r[p]),
        ))
        got_r[p] = make(right.at[1, part], right.at[0, part], perm_send.at[10 + p], perm_recv.at[0, p], pair)
        got_l[p] = make(left.at[1, part], left.at[0, part], perm_send.at[14 + p], perm_recv.at[0, 4 + p], pair)
    rstate_copy = send(rstate_ref, rstate, perm_send.at[8], perm_recv.at[0, 8], (lhs, next_r))
    lstate_copy = send(lstate_ref, lstate, perm_send.at[9], perm_recv.at[0, 9], (next_l, rhs))
    sent += [rstate_copy, lstate_copy]

    def relay(here, buffer, p, base, target):
        part, sem = pl.ds(*PIECES[p]), perm_send.at[10 + base + p]

        @pl.when(here)
        def _():
            make(buffer.at[0, part], buffer.at[1, part], sem, perm_recv.at[1, base + p], pair).wait_recv()
            make(buffer.at[1, part], buffer.at[0, part], sem, perm_recv.at[0, base + p], target).start()

    def relayed(here, buffer, p, base):
        part, sem = pl.ds(*PIECES[p]), perm_send.at[10 + base + p]

        @pl.when(here)
        def _():
            make(buffer.at[1, part], buffer.at[0, part], sem, perm_recv.at[0, base + p], pair).wait_send()

    relays = [
        (corner_r, right, 2, 0, (lhs, rhs - 3)),
        ((rhs % 4) == 0, right, 0, 0, (lhs, (rhs + 4) % 16)),
        (corner_l, left, 1, 4, (lhs - 15, rhs)),
        ((lhs % 16) == 13, left, 2, 4, (lhs - 13, rhs)),
        ((lhs % 16) == 2, left, 3, 4, (lhs - 2, rhs)),
        (corner_r, right, 3, 0, (lhs, rhs - 3)),
        ((rhs % 4) == 0, right, 1, 0, (lhs, (rhs + 4) % 16)),
    ]

    for load in loads[:6]:
        load.wait()
    rows8[0:1, :] = src_ref[...].astype(F32)
    rows8[1:2, :] = tgt_ref[...].astype(F32)
    rows8[2:3, :] = rel_ref[...].astype(F32)
    rows8[3:4, :] = neg_ref[...].astype(F32)
    rows8[4:8, :] = jnp.zeros((4, ROWS), F32)
    columns = rows8[...].T
    lane = lax.broadcasted_iota(jnp.int32, (ROWS, ROWS), 1).astype(F32)
    sublane = lax.broadcasted_iota(jnp.int32, (ROWS, ROWS), 0).astype(F32)
    hot_src = (columns[:, 0:1] == lane).astype(F32).astype(BF16)
    hot_src_t = (rows8[0:1, :] == sublane).astype(F32).astype(BF16)
    hot_tgt = (columns[:, 1:2] == lane).astype(F32)
    hot_neg = (columns[:, 3:4] == lane).astype(F32)
    multiplicity = jnp.sum(hot_neg, axis=0, keepdims=True)
    rel = rows8[2:3, :]
    edge = lax.broadcasted_iota(jnp.int32, (ROWS, 1), 0)
    live = (edge < cnt_ref[...]).astype(F32)
    state8[...] = jnp.zeros_like(state8)
    state8[0:2, 0:WIDTH] = opstate_ref[...]
    op_sums = state8[...].T
    tails[...] = jnp.zeros_like(tails)
    spare = jnp.zeros((4, 8, 128), F32)
    qy[6:8] = spare[0:2]
    qz[6:8] = spare[0:2]
    grad[0, 158:160] = spare[0:2]
    grad[1, 158:160] = spare[0:2]
    loads[6].wait()
    ops_split = [split(ops[r]) for r in range(2)]
    ops_t = [split(ops[r].T) for r in range(2)]

    for entry in relays:
        relay(*entry)

    in_high, in_low = [], []
    for p, part in enumerate(parts):
        got_l[2 * p].wait_recv()
        got_l[2 * p + 1].wait_recv()
        high, low = split(left[0, part, :])
        in_high.append(dot(high, hot_src_t).astype(BF16))
        in_low.append(dot(low, hot_src_t).astype(BF16))
    inputs = (jnp.concatenate(in_high, axis=0), jnp.concatenate(in_low, axis=0))
    mapped = jnp.where(rel < 0.5, dot3(ops_t[0], inputs), dot3(ops_t[1], inputs))
    inv_mapped = lax.rsqrt(jnp.sum(mapped * mapped, 0, keepdims=True) + 1e-06)
    unit_mapped = mapped * inv_mapped
    unit_rows = [split(unit_mapped[0:CUT].T), split(unit_mapped[CUT:WIDTH].T)]

    scores, square, right_split = 0.0, 0.0, []
    for p, part in enumerate(parts):
        got_r[2 * p].wait_recv()
        got_r[2 * p + 1].wait_recv()
        value = right[0, part, :]
        square = square + jnp.sum(value * value, 0, keepdims=True)
        right_split.append(split(value))
        scores = scores + dot3(unit_rows[p], right_split[p])
    inv_right = lax.rsqrt(square + 1e-06)
    scores = scores * inv_right
    positive = jnp.exp(jnp.sum(hot_tgt * scores, -1, keepdims=True))
    weights = multiplicity * jnp.exp(scores)
    norm = positive + jnp.sum(weights, -1, keepdims=True)
    scale = live / norm
    pull = weights * scale + hot_tgt * (positive * scale - live)
    pull_split = split(pull * inv_right)
    d_unit = jnp.concatenate([dot3(right_split[p], pull_split, NT) for p in range(2)], axis=0)
    d_mapped = inv_mapped * (d_unit - unit_mapped * jnp.sum(unit_mapped * d_unit, 0, keepdims=True))

    def operator_grad(kind, slot):
        high, low = split(jnp.where(rel == kind.astype(F32), d_mapped, 0.0))
        main = dot3(inputs, (high[0:ROWS], low[0:ROWS]), NT)
        for j in range(3):
            grad[slot, 50 * j:50 * j + 50] = main[:, 128 * j:128 * j + 128].reshape(50, 8, 128)
        tails[:, 0:WIDTH] = dot3((high[ROWS:WIDTH], low[ROWS:WIDTH]), inputs, NT)
        for i in range(2):
            for j in range(4):
                grad[slot, 150 + 4 * i + j] = tails[8 * i:8 * i + 8, 128 * j:128 * j + 128]

    operator_grad(other, 0)
    first = (("x", X0, XC, rx, 0), ("y", Y0, YC, ry, 3), ("z", Z0, ZC, rz, 10))
    pair_copies = []
    for part, (axis, start, count, _, _) in enumerate(first):
        span = pl.ds(start, count * size[axis])
        pair_copies.append(send(grad.at[0, span], sibling.at[span], core_send.at[part], core_recv.at[part], pair))
    operator_grad(mc, 1)
    copies1 = {}
    for part, (axis, start, count, slots, base) in enumerate(first):
        pair_copies[part].wait_recv()
        span = pl.ds(start, count * size[axis])
        total[span] = grad[1, span] + sibling[span]
        for steps in far(axis):
            to = (me[axis] + steps) % size[axis]
            k = base + steps - 1
            chunk = total.at[pl.ds(start + to * count, count)]
            copies1[k] = send(chunk, slots.at[steps - 1], s1.at[k], v1.at[k], along(axis, steps))

    rstate_copy.wait_recv()
    lstate_copy.wait_recv()
    unit_right = right[0] * inv_right
    d_right_unit = dot3(split(unit_mapped), split(pull))
    d_right = inv_right * (
        d_right_unit - unit_right * jnp.sum(unit_right * d_right_unit, 0, keepdims=True)
    )
    out_right[...] = adagrad(right[0], rstate[...], d_right, 0)
    right_out = pltpu.make_async_copy(out_right, new_right_ref, out_sem.at[0])
    right_out.start()
    d_inputs = dot3(ops_split[0], split(jnp.where(rel < 0.5, d_mapped, 0.0))) + dot3(
        ops_split[1], split(jnp.where(rel < 0.5, 0.0, d_mapped))
    )
    d_high, d_low = split(d_inputs)
    d_left = dot(d_high, hot_src) + dot(d_low, hot_src)
    out_left[...] = adagrad(left[0], lstate[...], d_left, 0)
    left_out = pltpu.make_async_copy(out_left, new_left_ref, out_sem.at[1])
    left_out.start()

    second = (("y", qx, r2x, 0, 2), ("x", qy, r2y, 7, 2), ("x", qz, r2z, 10, 2))
    copies2, copies3, copies4, copies5, copies6 = {}, {}, {}, {}, {}
    for part, (axis1, start, count, slots, base1) in enumerate(first):
        axis, pieces, slots2, base, many = second[part]
        for steps in range(1, size[axis1]):
            copies1[base1 + steps - 1].wait_recv()
        value = total[pl.ds(start + me[axis1] * count, count)]
        for slot in range(size[axis1] - 1):
            value = value + slots[slot]
        pieces[0:count] = value
        for steps in far(axis):
            to = (me[axis] + steps) % size[axis]
            k = base + steps - 1
            piece = pieces.at[pl.ds(to * many, many)]
            copies2[k] = send(piece, slots2.at[steps - 1], s2.at[k], v2.at[k], along(axis, steps))

    third = (("z", r3x, 0), ("z", r3y, 7), ("y", r3z, 14))
    for part in (0, 1, 2):
        axis2, pieces, slots2, base2, many = second[part]
        axis, slots, base = third[part]
        for steps in range(1, size[axis2]):
            copies2[base2 + steps - 1].wait_recv()
        value = pieces[pl.ds(me[axis2] * many, many)]
        for slot in range(size[axis2] - 1):
            value = value + slots2[slot]
        slots[me[axis]] = value
        for steps in far(axis):
            k = base + steps - 1
            slot = slots.at[me[axis]]
            copies3[k] = send(slot, slot, s3.at[k], v3.at[k], along(axis, steps))

    finals = (fx, fy, fz)
    for part in (0, 1, 2):
        axis3, slots, base3 = third[part]
        axis1 = first[part][0]
        axis2, _, _, base, many = second[part]
        for steps in range(1, size[axis3]):
            copies3[base3 + steps - 1].wait_recv()
        value = slots[0]
        for slot in range(1, size[axis3]):
            value = value + slots[slot]
        place = pl.ds(me[axis2] * many, many)
        finals[part][mc, me[axis1], place] = value
        piece = finals[part].at[mc, me[axis1], place]
        for steps in far(axis2):
            k = base + steps - 1
            copies4[k] = send(piece, piece, s4.at[k], v4.at[k], along(axis2, steps))

    for part in (0, 1, 2):
        axis1, _, count, _, base1 = first[part]
        axis2, _, _, base2, _ = second[part]
        for steps in range(1, size[axis2]):
            copies4[base2 + steps - 1].wait_recv()
        chunk = finals[part].at[mc, me[axis1], pl.ds(0, count)]
        for steps in far(axis1):
            k = base1 + steps - 1
            copies5[k] = send(chunk, chunk, s5.at[k], v5.at[k], along(axis1, steps))
        copies6[part] = send(chunk, chunk, s6.at[part], v6.at[part], pair)
    for part, (axis1, _, count, _, base1) in enumerate(first):
        for steps in sorted(range(1, size[axis1]), key=lambda d: min(d, size[axis1] - d)):
            k = base1 + steps - 1
            copies5[k].wait_recv()
            chunk = finals[part].at[mc, (me[axis1] + size[axis1] - steps) % size[axis1], pl.ds(0, count)]
            copies6[3 + k] = send(chunk, chunk, s6.at[3 + k], v6.at[3 + k], pair)
    ops_out = []
    for turn, kind in enumerate((mc, other)):
        for part, (axis1, start, count, _, base1) in enumerate(first):
            if turn:
                copies6[part].wait_recv()
                for steps in range(1, size[axis1]):
                    copies6[3 + base1 + steps - 1].wait_recv()
            for j in range(size[axis1]):
                for i in range(count):
                    unit = start + j * count + i
                    if unit < 150:
                        row, column = 8 * (unit % 50), 128 * (unit // 50)
                        gsum[row:row + 8, column:column + 128] = finals[part][kind, j, i]
                    elif unit < 158:
                        row, column = 8 * ((unit - 150) // 4), 128 * ((unit - 150) % 4)
                        tails[row:row + 8, column:column + 128] = finals[part][kind, j, i]
        gsum[:, ROWS:WIDTH] = tails[...].T[0:WIDTH]
        sums = jnp.where(kind == 0, op_sums[0:WIDTH, 0:1], op_sums[0:WIDTH, 1:2])
        out_ops[kind] = adagrad(ops[kind], sums, gsum[...], 1)
        ops_out.append(pltpu.make_async_copy(out_ops.at[kind], new_ops_ref.at[kind], out_sem.at[2 + turn]))
        ops_out[turn].start()
    for here, buffer, p, base, _ in relays:
        relayed(here, buffer, p, base)
    for copy in sent + pair_copies:
        copy.wait_send()
    for copies in (copies1, copies2, copies3, copies4, copies5, copies6):
        for copy in copies.values():
            copy.wait_send()
    right_out.wait()
    left_out.wait()
    ops_out[0].wait()
    ops_out[1].wait()


def hand_over(left_ref, right_ref, ops_ref, new_left_ref, new_right_ref, new_ops_ref, blocks, ops, sems):
    steps = []
    for i, (source, target) in enumerate(((left_ref, new_left_ref), (right_ref, new_right_ref))):
        for start in range(0, WIDTH, 200):
            part = pl.ds(start, 200)
            steps.append((source.at[part], blocks.at[i, part], target.at[part]))
    for kind in range(2):
        for start in range(0, WIDTH, 200):
            part = pl.ds(start, 200)
            steps.append((ops_ref.at[kind, part], ops.at[kind, part], new_ops_ref.at[kind, part]))
    loads = [pltpu.make_async_copy(a, b, sems.at[0, i]) for i, (a, b, _) in enumerate(steps)]
    stores = [pltpu.make_async_copy(b, c, sems.at[1, i]) for i, (_, b, c) in enumerate(steps)]
    for load in loads:
        load.start()
    for load, store in zip(loads, stores):
        load.wait()
        store.start()
    for store in stores:
        store.wait()


def body(
    left_table, left_state, right_table, right_state, operators, operator_state,
    sources, targets, relations, negatives, counts,
):
    hbm = pl.BlockSpec(memory_space=pl.ANY)
    dma = pltpu.SemaphoreType.DMA

    def buf(*shape):
        return pltpu.VMEM(shape, F32)

    def units(*shape):
        return pltpu.VMEM(shape + (8, 128), F32)

    block = jax.ShapeDtypeStruct((WIDTH, ROWS), F32)
    results = (block, block, jax.ShapeDtypeStruct((2, WIDTH, WIDTH), F32))
    trained = pl.pallas_call(
        kernel,
        out_shape=results,
        in_specs=[hbm] * 11,
        out_specs=(hbm, hbm, hbm),
        scratch_shapes=[
            buf(2, WIDTH, ROWS), buf(2, WIDTH, ROWS), buf(1, ROWS), buf(1, ROWS), buf(2, WIDTH, WIDTH),
            buf(WIDTH, ROWS), buf(WIDTH, ROWS), buf(2, WIDTH, WIDTH), buf(8, ROWS), buf(8, 512),
            buf(16, 512), buf(WIDTH, WIDTH),
            units(2, UNITS), units(UNITS), units(UNITS),
            units(3, XC), units(7, YC), units(7, ZC),
            units(XC), units(8), units(8),
            units(7, 2), units(3, 2), units(3, 2),
            units(8, 2), units(8, 2), units(8, 2),
            units(2, 4, XC), units(2, 8, 8), units(2, 8, 8),
            buf(2, WIDTH), *[pltpu.VMEM((1, ROWS), jnp.int32)] * 4, pltpu.VMEM((1, 1), jnp.int32),
            dma((18,)), dma((2, 10)), dma((7,)), dma((4,)),
            dma((3,)), dma((3,)), dma((17,)), dma((17,)), dma((13,)), dma((13,)),
            dma((21,)), dma((21,)), dma((13,)), dma((13,)), dma((17,)), dma((17,)),
            dma((20,)), dma((20,)),
        ],
        compiler_params=pltpu.CompilerParams(
            collective_id=0, has_side_effects=True, vmem_limit_bytes=VMEM_BYTES
        ),
        name="bucket_round",
    )(
        left_table.reshape(ROWS, WIDTH).T, left_state.reshape(1, ROWS),
        right_table.reshape(ROWS, WIDTH).T, right_state.reshape(1, ROWS),
        operators, operator_state,
        sources.reshape(1, ROWS), targets.reshape(1, ROWS),
        relations.reshape(1, ROWS), negatives.reshape(1, ROWS), counts,
    )
    new_left, new_right, new_operators = pl.pallas_call(
        hand_over,
        out_shape=results,
        in_specs=[hbm] * 3,
        out_specs=(hbm, hbm, hbm),
        scratch_shapes=[buf(2, WIDTH, ROWS), buf(2, WIDTH, WIDTH), dma((2, 8))],
        compiler_params=pltpu.CompilerParams(vmem_limit_bytes=VMEM_BYTES),
        name="hand_over",
    )(*trained)
    return new_left.T[None, None], new_right.T[None, None], new_operators


def solution(mesh):
    edges = P("lhs", "rhs", None)
    blocks = P("lhs", "rhs", None, None)
    return jax.shard_map(
        body,
        mesh=mesh,
        in_specs=(blocks, edges, blocks, edges, P(), P(), edges, edges, edges, edges, P("lhs", "rhs")),
        out_specs=(blocks, blocks, P()),
        check_vma=False,
    )
```
